32 devices in a mesh: rep: 2 (over y), tp: 4 (over z), pd: 2 (over x), st: 2 (over core).
Axes of the slice: x: 2, y: 2, z: 4, core: 2. Of those that a mesh axis runs over, the one named last changes fastest.
Arguments:
- tokens: bfloat16 [4096, 8192], P(('rep', 'pd', 'st'), 'tp'), parts along dimension 0, may hold values from -6 to 6
- key_value_matrix: bfloat16 [8192, 2048], P('tp'), may hold values from -0.09375 to 0.09375
- adapter_down_weight: bfloat16 [128, 8192, 128], P(('rep', 'pd', 'st'), 'tp'), parts along dimension 0, may hold values from -0.0625 to 0.0625
- adapter_up_weight: bfloat16 [128, 64, 2048], P(('rep', 'pd', 'st'), None, 'tp'), parts along dimension 0, may hold values from -0.75 to 0.75
- adapter_store_slot: int32 [128], P('rep'), parts along dimension 0, may hold values from 0 to 63, as said below
- request_adapter: int32 [8, 8], P(('rep', 'pd', 'st')), parts along dimension 0, may hold values from 0 to 63, as said below
- prefill_span_pages: int32 [8, 8], P(('rep', 'pd', 'st')), parts along dimension 0, may hold values from 1 to 16, 32 in all within a row
- decode_pool_slot: int32 [8, 32], P('rep'), parts along dimension 0, may hold values from 0 to 127, as said below
Outputs:
- decode_pool: bfloat16 [256, 16, 2048], P(('rep', 'pd', 'st'), None, 'tp'), parts along dimension 0
The draws below stay inside these ranges and needn't reach their ends.
There are 2 independent parts, one for each index of `rep`. The reference program is written for one: setup_inputs(seed, part) draws one part's arguments, and reference() takes and returns one part's arrays. A program takes and returns all parts, laid end to end along the dimension named above; an argument that names none is the same for every part. Nothing has to cross between parts.
Inputs may be any that keep to these rules, and one draw needn't show every extreme that they name: `adapter_store_slot`: a permutation of the store slots; slot s lies on the store device with index s // 16 of the joined axes pd and st. `request_adapter`: no group asks more than 3 of its requests from one store device, and every group asks exactly 3 from some store device. `prefill_span_pages`: each row sums to 32, its largest entry is 16. `decode_pool_slot`: a permutation of the pool slots; the pages of group g go to pools of groups that differ from g only in their pd index.
All inputs are finite; a program needn't handle non-finite values.
Results may differ from the reference program's by a relative error of at most 0.006.
Values may be sent and summed in bfloat16 or wider, within the bound.
A program may use at most 128 MiB of HBM per device.

```python
import math
import jax
import jax.numpy as jnp
import numpy as np
from jax import lax

MODEL_WIDTH = 8192
ADAPTER_RANK = 64
PAGE_TOKENS = 16
PG = 32
REQ_DEV = 8
ADAPT_DEV = 16
KEY_VALUE_WIDTH = 2048
LEN_MOST = 16
GROUPS = 4
TOKENS = 2048
POOL_PAGES = 128
ADAPTER_COUNT = 64
N_PD = 2
N_ST = 2


def store_order(key):
    return jax.random.permutation(key, ADAPTER_COUNT)


def draw_adapter_store_slot(key, part):
    placement = store_order(key)
    return placement.astype(jnp.int32)


def draw_request_adapter(key, part):
    placement = store_order(key)
    key = jax.random.fold_in(key, 2)
    inverse = jnp.argsort(placement)
    key_one, key_two, key_three, key_four = jax.random.split(key, 4)
    offset = jax.random.randint(key_one, (GROUPS, 1), 0, GROUPS)
    holders = (jnp.arange(REQ_DEV)[None, :] + offset) % GROUPS
    holders = holders.at[:, 1].set(holders[:, 0])
    coin = jax.random.randint(key_two, (GROUPS,), 0, 2)
    holders = holders.at[:, 3].set(jnp.where(coin == 1, holders[:, 2], holders[:, 3]))
    order = jax.vmap(lambda sub: jax.random.permutation(sub, REQ_DEV))(jax.random.split(key_three, GROUPS))
    holders = jnp.take_along_axis(holders, order, axis=1)
    within = jax.random.randint(key_four, (GROUPS, REQ_DEV), 0, ADAPT_DEV)
    return inverse[holders * ADAPT_DEV + within].astype(jnp.int32)


def draw_decode_pool_slot(key, part):
    key = jax.random.fold_in(key, 3)
    orders = jax.vmap(lambda sub: jax.random.permutation(sub, N_PD * PG))(jax.random.split(key, N_ST))
    source_pd = jnp.arange(N_PD)[:, None, None]
    st_index = jnp.arange(N_ST)[None, :, None]
    page_index = jnp.arange(PG)[None, None, :]
    flattened_index = source_pd * PG + page_index
    target = orders[st_index, flattened_index]
    global_slot = (target // PG * N_ST + st_index) * PG + target % PG
    return global_slot.reshape(GROUPS, PG).astype(jnp.int32)


def with_spikes(drawn, own_key, source, target, blocks, factor):
    owner, partner = [(jnp.arange(drawn.shape[position]) // (drawn.shape[position] // blocks)).reshape([-1 if axis == position else 1 for axis in range(drawn.ndim)]) for position in (source, target)]
    chosen = jax.random.permutation(own_key, blocks)[partner]
    strong = (owner == chosen) | (owner == (partner + blocks // 2) % blocks)
    return jnp.where(strong, factor * drawn, drawn)


def steps_of(key, dims, pieces, smallest, high):
    factor_of, own = 1.0, jax.random.fold_in(key, 6)
    for axis_at, parts in pieces:
        steps = jnp.exp(jax.random.uniform(jax.random.fold_in(own, axis_at), (parts,), jnp.float32, smallest / len(pieces), high / len(pieces)))
        factor_of = factor_of * jnp.repeat(steps, dims[axis_at] // parts).reshape([-1 if axis == axis_at else 1 for axis in range(len(dims))])
    return factor_of


def length_profile(number_of, total, reach, lean):
    weights = [(1 << 20) // math.isqrt(standing ** lean) + 1 for standing in range(2, number_of + 1)]
    rest, counts = total - reach - (number_of - 1), [1] * (number_of - 1)
    while rest > 0:
        movable = [i for i in range(number_of - 1) if counts[i] < reach]
        whole, remaining = sum([weights[i] for i in movable]), rest
        for i in movable:
            addition = min(reach - counts[i], max(1, remaining * weights[i] // whole), rest)
            counts[i] = counts[i] + addition
            rest = rest - addition
    return np.array([reach] + counts)


def ragged_sizes(stream_key, number_of, total, limit, skew):
    if number_of == 2:
        one = jax.random.randint(stream_key, (), max(1, total - limit), min(limit, total - 1) + 1)
        return jnp.stack([one, total - one])
    sizes = jnp.asarray(length_profile(number_of, total, limit, skew), jnp.int32)
    pairs = (number_of - 1) // 2
    donor, taker = sizes[1:1 + 2 * pairs:2], sizes[2:2 + 2 * pairs:2]
    room = jnp.minimum(donor - 1, limit - taker)
    shifted = jax.random.randint(jax.random.fold_in(stream_key, 1), (pairs,), 0, 1 << 20) % (room + 1)
    sizes = sizes.at[1:1 + 2 * pairs:2].set(donor - shifted).at[2:2 + 2 * pairs:2].set(taker + shifted)
    return sizes[jax.random.permutation(jax.random.fold_in(stream_key, 2), number_of)]


def gaussian(own_key, extent, spread, limit, cuts=(), kind=jnp.bfloat16):
    drawn = jax.random.normal(own_key, extent, jnp.float32) * spread
    if len(cuts) > 0:
        drawn = steps_of(own_key, extent, cuts, -0.22, 0.18) * drawn
    return jnp.clip(drawn, min=-limit, max=limit).astype(kind)


def gaussian_with(rng, dims, width, limit, shards, heavy, held_as=jnp.bfloat16):
    entries = width * jax.random.normal(rng, dims, jnp.float32)
    if shards:
        entries = entries * steps_of(rng, dims, shards, -0.22, 0.18)
    return jnp.clip(with_spikes(entries, jax.random.fold_in(rng, 3), *heavy), -limit, limit).astype(held_as)


def setup_inputs(seed: int = 0, part: int = 0) -> dict:
    arg_keys = jax.random.split(jax.random.key(seed), 9)
    part_keys = jax.random.split(jax.random.fold_in(arg_keys[8], part), 9)
    tokens = gaussian(part_keys[0], (TOKENS, MODEL_WIDTH), 1.0, 6.0, ((0, 4), (1, 4)))
    key_value_matrix = gaussian_with(arg_keys[1], (MODEL_WIDTH, KEY_VALUE_WIDTH), MODEL_WIDTH ** -0.5, 0.09375, ((0, 4),), (0, 1, 4, 2.0))
    adapter_down_weight = gaussian(part_keys[2], (ADAPTER_COUNT, MODEL_WIDTH, 2 * ADAPTER_RANK), MODEL_WIDTH ** -0.5, 0.0625, ((0, 4), (1, 4)))
    adapter_up_weight = gaussian(part_keys[3], (ADAPTER_COUNT, ADAPTER_RANK, KEY_VALUE_WIDTH), ADAPTER_RANK ** -0.5, 0.75, ((0, 4), (2, 4)))
    adapter_store_slot = draw_adapter_store_slot(jax.random.fold_in(jax.random.fold_in(arg_keys[8], part), 71), part)
    request_adapter = draw_request_adapter(jax.random.fold_in(jax.random.fold_in(arg_keys[8], part), 71), part)
    prefill_span_pages = jax.vmap(lambda own: ragged_sizes(own, REQ_DEV, PG, LEN_MOST, 2))(jax.random.split(part_keys[6], GROUPS)).reshape((GROUPS, REQ_DEV)).astype(jnp.int32)
    decode_pool_slot = draw_decode_pool_slot(jax.random.fold_in(jax.random.fold_in(arg_keys[8], part), 71), part)
    return {"tokens": tokens, "key_value_matrix": key_value_matrix, "adapter_down_weight": adapter_down_weight, "adapter_up_weight": adapter_up_weight, "adapter_store_slot": adapter_store_slot, "request_adapter": request_adapter, "prefill_span_pages": prefill_span_pages, "decode_pool_slot": decode_pool_slot}


adapter_scale = 0.5


def reference(tokens, key_value_matrix, adapter_down_weight, adapter_up_weight, adapter_store_slot, request_adapter, prefill_span_pages, decode_pool_slot):
    base_output = jnp.dot(tokens, key_value_matrix, preferred_element_type=jnp.float32)
    page_ends = jnp.cumsum(prefill_span_pages, axis=1)
    page_index = jnp.arange(PG, dtype=jnp.int32)
    request_of_page = jnp.sum((page_ends[:, None, :] <= page_index[None, :, None]).astype(jnp.int32), axis=2).astype(jnp.int32)
    page_adapter = jnp.take_along_axis(request_adapter, request_of_page, axis=1).reshape(-1).astype(jnp.int32)
    page_store = jnp.take(adapter_store_slot, page_adapter).astype(jnp.int32)
    token_pages = tokens.reshape(POOL_PAGES, PAGE_TOKENS, MODEL_WIDTH)
    half_width = KEY_VALUE_WIDTH // 2

    def one_page(items):
        rows, store_position = items
        down_single_page = lax.dynamic_index_in_dim(adapter_down_weight, store_position, 0, keepdims=False)
        up_single_page = lax.dynamic_index_in_dim(adapter_up_weight, store_position, 0, keepdims=False).astype(jnp.float32)
        inner = jnp.dot(rows, down_single_page, preferred_element_type=jnp.float32)
        delta_key = jnp.dot(inner[:, :ADAPTER_RANK], up_single_page[:, :half_width], precision=lax.Precision.HIGHEST)
        delta_value = jnp.dot(inner[:, ADAPTER_RANK:], up_single_page[:, half_width:], precision=lax.Precision.HIGHEST)
        return jnp.concatenate([delta_key, delta_value], axis=1)

    update_term = lax.map(one_page, (token_pages, page_store)).reshape(TOKENS, KEY_VALUE_WIDTH)
    key_value_rows = (base_output + adapter_scale * update_term).astype(jnp.bfloat16).reshape(POOL_PAGES, PAGE_TOKENS, KEY_VALUE_WIDTH)
    return jnp.zeros_like(key_value_rows).at[decode_pool_slot.reshape(-1)].set(key_value_rows)
```

```python
import functools

import jax
import jax.numpy as jnp
from jax import lax
from jax.experimental import pallas as pl
from jax.experimental.pallas import tpu as pltpu
from jax.sharding import PartitionSpec as P

PAGE_TOKENS = 16
CHUNK_PAGES = 8


adapter_scale = 0.5


def down_kernel(sources, requests, slots, starts, counts, down, *refs):
    rows, outs = refs[:sources], refs[sources:]
    page_count = rows[0].shape[0] // PAGE_TOKENS
    chunk_rows = CHUNK_PAGES * PAGE_TOKENS
    for source in range(sources):
        outs[source][...] = jnp.zeros_like(outs[source])

        @pl.loop(0, requests)
        def _(request):
            slot = slots[source, request]
            start = starts[source, request]
            count = counts[source, request]

            @pl.when(slot >= 0)
            def _():
                @pl.loop(0, (count + CHUNK_PAGES - 1) // CHUNK_PAGES)
                def _(chunk):
                    first = jnp.minimum(start + chunk * CHUNK_PAGES, page_count - CHUNK_PAGES)
                    place = pl.ds(pl.multiple_of(first * PAGE_TOKENS, PAGE_TOKENS), chunk_rows)
                    product = jnp.dot(
                        rows[source][place, :], down[slot], preferred_element_type=jnp.float32
                    )
                    row = first * PAGE_TOKENS + lax.broadcasted_iota(jnp.int32, product.shape, 0)
                    inside = (row >= start * PAGE_TOKENS) & (row < (start + count) * PAGE_TOKENS)
                    held = outs[source][place, :].astype(jnp.float32)
                    outs[source][place, :] = jnp.where(inside, product, held).astype(jnp.bfloat16)


def down_products(row_list, slots, starts, counts, down):
    sources, requests = slots.shape
    token_rows, width = row_list[0].shape
    rank = down.shape[2]
    in_vmem = pl.BlockSpec(memory_space=pltpu.VMEM)
    in_smem = pl.BlockSpec(memory_space=pltpu.SMEM)
    return pl.pallas_call(
        functools.partial(down_kernel, sources, requests),
        out_shape=[jax.ShapeDtypeStruct((token_rows, rank), jnp.bfloat16)] * sources,
        in_specs=[in_smem] * 3 + [in_vmem] * (1 + sources),
        out_specs=[in_vmem] * sources,
        compiler_params=pltpu.CompilerParams(vmem_limit_bytes=40 * 1024 * 1024),
        cost_estimate=pl.CostEstimate(
            flops=2 * sources * token_rows * width * rank,
            bytes_accessed=2 * (down.size + sources * token_rows * (width + rank)),
            transcendentals=0,
        ),
        name="down_products",
    )(slots, starts, counts, down, *row_list)


def shifted(value, axis, step):
    size = lax.axis_size(axis)
    return lax.ppermute(value, axis, [(i, (i + step) % size) for i in range(size)])


def on_device(
    tokens,
    key_value_matrix,
    adapter_down_weight,
    adapter_up_weight,
    adapter_store_slot,
    request_adapter,
    prefill_span_pages,
    decode_pool_slot,
):
    pd_count = lax.axis_size("pd")
    st_count = lax.axis_size("st")
    pd_index = lax.axis_index("pd")
    st_index = lax.axis_index("st")
    groups = pd_count * st_count
    me = pd_index * st_count + st_index
    adapter_rank_value = adapter_up_weight.shape[1]
    column_range = adapter_up_weight.shape[2]
    requests = request_adapter.shape[1]
    slot_capacity = requests // groups + 1
    holding_count = adapter_down_weight.shape[0]
    token_rows = tokens.shape[0]
    page_count = token_rows // PAGE_TOKENS

    travelled = {(0, 0): tokens}
    for step in range(1, pd_count):
        travelled[step, 0] = shifted(tokens, "pd", step)
    for step in range(pd_count):
        for turn in range(1, st_count):
            travelled[step, turn] = shifted(travelled[step, 0], "st", turn)

    asked = jnp.concatenate([request_adapter, prefill_span_pages], axis=1)
    asked = lax.all_gather(asked, ("pd", "st"), axis=0, tiled=True)
    store_slot = jnp.take(adapter_store_slot, asked[:, :requests])
    counts = asked[:, requests:]
    ends = jnp.cumsum(counts, axis=1)
    starts = ends - counts
    holder = store_slot // holding_count
    local_index = store_slot % holding_count
    own_slot = jnp.where(holder == me, local_index, -1)

    base_part = jnp.dot(tokens, key_value_matrix, preferred_element_type=jnp.float32)
    base_sum = lax.psum_scatter(
        base_part.astype(jnp.bfloat16), "tp", scatter_dimension=1, tiled=True
    )

    order_ids = jnp.arange(requests)
    earlier = (holder[:, None, :] == holder[:, :, None]) & (
        order_ids[None, None, :] < order_ids[None, :, None]
    )
    rank_in = jnp.sum(earlier.astype(jnp.int32), axis=2)
    hits = (holder == me)[:, :, None] & (
        rank_in[:, :, None] == jnp.arange(slot_capacity)[None, None, :]
    )
    asked_pages = jnp.sum(jnp.where(hits, local_index[:, :, None], 0), axis=1).reshape(-1)
    up_page_list = jnp.take(adapter_up_weight, asked_pages, axis=0, mode="clip").reshape(
        groups, slot_capacity, adapter_rank_value, column_range
    )
    arrived_up = lax.all_to_all(
        up_page_list, ("pd", "st"), split_axis=0, concat_axis=0, tiled=True
    )
    own_holder = lax.dynamic_index_in_dim(holder, me, 0, keepdims=False)
    own_rank = lax.dynamic_index_in_dim(rank_in, me, 0, keepdims=False)
    own_ends = lax.dynamic_index_in_dim(ends, me, 0, keepdims=False)
    request_of_page = jnp.sum(
        (own_ends[None, :] <= jnp.arange(page_count)[:, None]).astype(jnp.int32), axis=1
    )
    source_of_page = jnp.take(own_holder * slot_capacity + own_rank, request_of_page, mode="clip")
    page_up_weight = jnp.take(
        arrived_up.reshape(groups * slot_capacity, adapter_rank_value, column_range),
        source_of_page,
        axis=0,
        mode="clip",
    )

    inner = None
    for step in range(pd_count):
        source_group = jnp.stack(
            [
                (pd_index - step) % pd_count * st_count + (st_index - turn) % st_count
                for turn in range(st_count)
            ]
        )
        products = down_products(
            [travelled[step, turn] for turn in range(st_count)],
            jnp.take(own_slot, source_group, axis=0, mode="clip"),
            jnp.take(starts, source_group, axis=0, mode="clip"),
            jnp.take(counts, source_group, axis=0, mode="clip"),
            adapter_down_weight,
        )
        chip_sum = products[0]
        for turn in range(1, st_count):
            chip_sum = chip_sum + shifted(products[turn], "st", -turn)
        returned = chip_sum if step == 0 else shifted(chip_sum, "pd", -step)
        inner = returned if inner is None else inner + returned

    adapter_whole = lax.psum(inner, "tp").reshape(page_count, PAGE_TOKENS, -1)
    half_tensor_parallel = lax.axis_size("tp") // 2
    halfway_start = jnp.where(lax.axis_index("tp") >= half_tensor_parallel, adapter_rank_value, 0)
    adapter_halfway = lax.dynamic_slice_in_dim(adapter_whole, halfway_start, adapter_rank_value, 2)
    update = jnp.einsum(
        "ueo,uox->uex", adapter_halfway, page_up_weight, preferred_element_type=jnp.float32
    )
    completed = base_sum.astype(jnp.float32).reshape(update.shape) + adapter_scale * update
    pages = completed.astype(jnp.bfloat16).reshape(page_count, PAGE_TOKENS * column_range)

    slot_table = decode_pool_slot.reshape(pd_count, st_count, page_count)
    slot_table = lax.dynamic_index_in_dim(slot_table, st_index, 1, keepdims=False)
    own_slots = me * page_count + jnp.arange(page_count)
    decode_pool = None
    for step in range(pd_count):
        arrived = pages if step == 0 else shifted(pages, "pd", step)
        dest = lax.dynamic_index_in_dim(
            slot_table, (pd_index - step) % pd_count, 0, keepdims=False
        )
        selector = (dest[None, :] == own_slots[:, None]).astype(jnp.bfloat16)
        picked = jnp.dot(selector, arrived, preferred_element_type=jnp.float32)
        decode_pool = picked if decode_pool is None else decode_pool + picked
    return decode_pool.astype(jnp.bfloat16).reshape(page_count, PAGE_TOKENS, column_range)


def solution(mesh):
    placed = (
        P(("rep", "pd", "st"), "tp"),
        P("tp", None),
        P(("rep", "pd", "st"), "tp", None),
        P(("rep", "pd", "st"), None, "tp"),
        P("rep"),
        P(("rep", "pd", "st"), None),
        P(("rep", "pd", "st"), None),
        P("rep", None),
    )
    return jax.shard_map(
        on_device,
        mesh=mesh,
        in_specs=placed,
        out_specs=P(("rep", "pd", "st"), None, "tp"),
        check_vma=False,
    )
```

```python
import functools

import jax
import jax.numpy as jnp
from jax import lax
from jax.experimental import pallas as pl
from jax.experimental.pallas import tpu as pltpu
from jax.sharding import PartitionSpec as P

PAGE_TOKENS = 16
CHUNK_PAGES = 8


adapter_scale = 0.5


def down_kernel(sources, requests, slots, starts, counts, down, *refs):
    rows, outs = refs[:sources], refs[sources:]
    page_count = rows[0].shape[0] // PAGE_TOKENS
    chunk_rows = CHUNK_PAGES * PAGE_TOKENS
    for source in range(sources):
        outs[source][...] = jnp.zeros_like(outs[source])

        @pl.loop(0, requests)
        def _(request):
            slot = slots[source, request]
            start = starts[source, request]
            count = counts[source, request]

            @pl.when(slot >= 0)
            def _():
                @pl.loop(0, (count + CHUNK_PAGES - 1) // CHUNK_PAGES)
                def _(chunk):
                    first = jnp.minimum(start + chunk * CHUNK_PAGES, page_count - CHUNK_PAGES)
                    place = pl.ds(pl.multiple_of(first * PAGE_TOKENS, PAGE_TOKENS), chunk_rows)
                    product = jnp.dot(
                        rows[source][place, :], down[slot], preferred_element_type=jnp.float32
                    )
                    row = first * PAGE_TOKENS + lax.broadcasted_iota(jnp.int32, product.shape, 0)
                    inside = (row >= start * PAGE_TOKENS) & (row < (start + count) * PAGE_TOKENS)
                    held = outs[source][place, :].astype(jnp.float32)
                    outs[source][place, :] = jnp.where(inside, product, held).astype(jnp.bfloat16)


def down_products(row_list, slots, starts, counts, down):
    sources, requests = slots.shape
    token_rows, width = row_list[0].shape
    rank = down.shape[2]
    in_vmem = pl.BlockSpec(memory_space=pltpu.VMEM)
    in_smem = pl.BlockSpec(memory_space=pltpu.SMEM)
    return pl.pallas_call(
        functools.partial(down_kernel, sources, requests),
        out_shape=[jax.ShapeDtypeStruct((token_rows, rank), jnp.bfloat16)] * sources,
        in_specs=[in_smem] * 3 + [in_vmem] * (1 + sources),
        out_specs=[in_vmem] * sources,
        compiler_params=pltpu.CompilerParams(vmem_limit_bytes=40 * 1024 * 1024),
        cost_estimate=pl.CostEstimate(
            flops=2 * sources * token_rows * width * rank,
            bytes_accessed=2 * (down.size + sources * token_rows * (width + rank)),
            transcendentals=0,
        ),
        name="down_products",
    )(slots, starts, counts, down, *row_list)


def shifted(value, axis, step):
    size = lax.axis_size(axis)
    return lax.ppermute(value, axis, [(i, (i + step) % size) for i in range(size)])


def on_device(
    tokens,
    key_value_matrix,
    adapter_down_weight,
    adapter_up_weight,
    adapter_store_slot,
    request_adapter,
    prefill_span_pages,
    decode_pool_slot,
):
    pd_count = lax.axis_size("pd")
    st_count = lax.axis_size("st")
    pd_index = lax.axis_index("pd")
    st_index = lax.axis_index("st")
    groups = pd_count * st_count
    me = pd_index * st_count + st_index
    adapter_rank_value = adapter_up_weight.shape[1]
    column_range = adapter_up_weight.shape[2]
    requests = request_adapter.shape[1]
    slot_capacity = requests // groups + 1
    holding_count = adapter_down_weight.shape[0]
    token_rows = tokens.shape[0]
    page_count = token_rows // PAGE_TOKENS

    travelled = {(0, 0): tokens}
    for step in range(1, pd_count):
        travelled[step, 0] = shifted(tokens, "pd", step)
    for turn in range(1, st_count):
        travelled[0, turn] = shifted(tokens, "st", turn)

    tokens, near_other = lax.optimization_barrier(
        (tokens, [travelled[0, turn] for turn in range(1, st_count)])
    )
    for turn in range(1, st_count):
        travelled[0, turn] = near_other[turn - 1]
    base_part = jnp.dot(tokens, key_value_matrix, preferred_element_type=jnp.float32)
    base_part, request_adapter, prefill_span_pages = lax.optimization_barrier(
        (base_part.astype(jnp.bfloat16), request_adapter, prefill_span_pages)
    )
    base_sum = lax.psum_scatter(base_part, "tp", scatter_dimension=1, tiled=True)

    asked = jnp.concatenate([request_adapter, prefill_span_pages], axis=1)
    asked = lax.all_gather(asked, ("pd", "st"), axis=0, tiled=True)
    store_slot = jnp.take(adapter_store_slot, asked[:, :requests])
    counts = asked[:, requests:]
    ends = jnp.cumsum(counts, axis=1)
    starts = ends - counts
    holder = store_slot // holding_count
    local_index = store_slot % holding_count
    own_slot = jnp.where(holder == me, local_index, -1)

    order_ids = jnp.arange(requests)
    earlier = (holder[:, None, :] == holder[:, :, None]) & (
        order_ids[None, None, :] < order_ids[None, :, None]
    )
    rank_in = jnp.sum(earlier.astype(jnp.int32), axis=2)
    hits = (holder == me)[:, :, None] & (
        rank_in[:, :, None] == jnp.arange(slot_capacity)[None, None, :]
    )
    asked_pages = jnp.sum(jnp.where(hits, local_index[:, :, None], 0), axis=1).reshape(-1)
    up_page_list = jnp.take(adapter_up_weight, asked_pages, axis=0, mode="clip").reshape(
        groups, slot_capacity, adapter_rank_value, column_range
    )
    arrived_up = lax.all_to_all(
        up_page_list, ("pd", "st"), split_axis=0, concat_axis=0, tiled=True
    )
    own_holder = lax.dynamic_index_in_dim(holder, me, 0, keepdims=False)
    own_rank = lax.dynamic_index_in_dim(rank_in, me, 0, keepdims=False)
    own_ends = lax.dynamic_index_in_dim(ends, me, 0, keepdims=False)
    request_of_page = jnp.sum(
        (own_ends[None, :] <= jnp.arange(page_count)[:, None]).astype(jnp.int32), axis=1
    )
    source_of_page = jnp.take(own_holder * slot_capacity + own_rank, request_of_page, mode="clip")
    page_up_weight = jnp.take(
        arrived_up.reshape(groups * slot_capacity, adapter_rank_value, column_range),
        source_of_page,
        axis=0,
        mode="clip",
    )

    def request_tables(step):
        source_group = jnp.stack(
            [
                (pd_index - step) % pd_count * st_count + (st_index - turn) % st_count
                for turn in range(st_count)
            ]
        )
        tables = [
            jnp.take(table, source_group, axis=0, mode="clip")
            for table in (own_slot, starts, counts)
        ]
        return tables

    def summed_products(tables, row_list):
        products = down_products(row_list, *tables, adapter_down_weight)
        chip_sum = products[0]
        for turn in range(1, st_count):
            chip_sum = chip_sum + shifted(products[turn], "st", -turn)
        return chip_sum

    near_rows = [travelled[0, turn] for turn in range(st_count)]
    inner = summed_products(request_tables(0), near_rows).astype(jnp.float32)
    far_tables = [request_tables(step) for step in range(1, pd_count)]
    far_rows = [travelled[step, 0] for step in range(1, pd_count)]
    inner, page_up_weight, base_sum, far_tables, far_rows = lax.optimization_barrier(
        (inner, page_up_weight, base_sum, far_tables, far_rows)
    )
    for step in range(1, pd_count):
        rows = far_rows[step - 1]
        row_list = [rows] + [shifted(rows, "st", turn) for turn in range(1, st_count)]
        returned = shifted(summed_products(far_tables[step - 1], row_list), "pd", -step)
        inner = inner + returned

    tp_count = lax.axis_size("tp")
    half_tensor_parallel = tp_count // 2
    upper = lax.axis_index("tp") >= half_tensor_parallel
    half_rows = token_rows // 2

    def packed(columns):
        return jnp.concatenate([columns[:half_rows], columns[half_rows:]], axis=1)

    first, second = packed(inner[:, :adapter_rank_value]), packed(inner[:, adapter_rank_value:])
    mine = jnp.where(upper, second, first)
    theirs = jnp.where(upper, first, second).astype(jnp.bfloat16)
    mine = mine + shifted(theirs, "tp", half_tensor_parallel)
    distance = half_tensor_parallel // 2
    while distance >= 1:
        pairs = [(i, i ^ distance) for i in range(tp_count)]
        mine = mine + lax.ppermute(mine.astype(jnp.bfloat16), "tp", pairs)
        distance //= 2
    mine = mine.astype(jnp.bfloat16)
    adapter_halfway = jnp.concatenate(
        [mine[:, :adapter_rank_value], mine[:, adapter_rank_value:]], axis=0
    ).reshape(page_count, PAGE_TOKENS, adapter_rank_value)
    update = jnp.einsum(
        "ueo,uox->uex", adapter_halfway, page_up_weight, preferred_element_type=jnp.float32
    )
    completed = base_sum.astype(jnp.float32).reshape(update.shape) + adapter_scale * update
    pages = completed.astype(jnp.bfloat16).reshape(page_count, PAGE_TOKENS * column_range)

    slot_table = decode_pool_slot.reshape(pd_count, st_count, page_count)
    slot_table = lax.dynamic_index_in_dim(slot_table, st_index, 1, keepdims=False)
    own_slots = me * page_count + jnp.arange(page_count)
    decode_pool = None
    for step in range(pd_count):
        arrived = pages if step == 0 else shifted(pages, "pd", step)
        dest = lax.dynamic_index_in_dim(
            slot_table, (pd_index - step) % pd_count, 0, keepdims=False
        )
        selector = (dest[None, :] == own_slots[:, None]).astype(jnp.bfloat16)
        picked = jnp.dot(selector, arrived, preferred_element_type=jnp.float32)
        decode_pool = picked if decode_pool is None else decode_pool + picked
    return decode_pool.astype(jnp.bfloat16).reshape(page_count, PAGE_TOKENS, column_range)


def solution(mesh):
    placed = (
        P(("rep", "pd", "st"), "tp"),
        P("tp", None),
        P(("rep", "pd", "st"), "tp", None),
        P(("rep", "pd", "st"), None, "tp"),
        P("rep"),
        P(("rep", "pd", "st"), None),
        P(("rep", "pd", "st"), None),
        P("rep", None),
    )
    return jax.shard_map(
        on_device,
        mesh=mesh,
        in_specs=placed,
        out_specs=P(("rep", "pd", "st"), None, "tp"),
        check_vma=False,
    )
```

```python
import functools

import jax
import jax.numpy as jnp
from jax import lax
from jax.experimental import pallas as pl
from jax.experimental.pallas import tpu as pltpu
from jax.sharding import PartitionSpec as P

PAGE_TOKENS = 16
CHUNK_PAGES = 8


adapter_scale = 0.5


def down_kernel(sources, requests, slots, starts, counts, down, *refs):
    rows, outs = refs[:sources], refs[sources:]
    page_count = rows[0].shape[0] // PAGE_TOKENS
    chunk_rows = CHUNK_PAGES * PAGE_TOKENS
    for source in range(sources):
        outs[source][...] = jnp.zeros_like(outs[source])

        @pl.loop(0, requests)
        def _(request):
            slot = slots[source, request]
            start = starts[source, request]
            count = counts[source, request]

            @pl.when(slot >= 0)
            def _():
                @pl.loop(0, (count + CHUNK_PAGES - 1) // CHUNK_PAGES)
                def _(chunk):
                    first = jnp.minimum(start + chunk * CHUNK_PAGES, page_count - CHUNK_PAGES)
                    place = pl.ds(pl.multiple_of(first * PAGE_TOKENS, PAGE_TOKENS), chunk_rows)
                    product = jnp.dot(
                        rows[source][place, :], down[slot], preferred_element_type=jnp.float32
                    )
                    row = first * PAGE_TOKENS + lax.broadcasted_iota(jnp.int32, product.shape, 0)
                    inside = (row >= start * PAGE_TOKENS) & (row < (start + count) * PAGE_TOKENS)
                    held = outs[source][place, :].astype(jnp.float32)
                    outs[source][place, :] = jnp.where(inside, product, held).astype(jnp.bfloat16)


def down_products(row_list, slots, starts, counts, down):
    sources, requests = slots.shape
    token_rows, width = row_list[0].shape
    rank = down.shape[2]
    in_vmem = pl.BlockSpec(memory_space=pltpu.VMEM)
    in_smem = pl.BlockSpec(memory_space=pltpu.SMEM)
    return pl.pallas_call(
        functools.partial(down_kernel, sources, requests),
        out_shape=[jax.ShapeDtypeStruct((token_rows, rank), jnp.bfloat16)] * sources,
        in_specs=[in_smem] * 3 + [in_vmem] * (1 + sources),
        out_specs=[in_vmem] * sources,
        compiler_params=pltpu.CompilerParams(vmem_limit_bytes=40 * 1024 * 1024),
        cost_estimate=pl.CostEstimate(
            flops=2 * sources * token_rows * width * rank,
            bytes_accessed=2 * (down.size + sources * token_rows * (width + rank)),
            transcendentals=0,
        ),
        name="down_products",
    )(slots, starts, counts, down, *row_list)


def shifted(value, axis, step):
    size = lax.axis_size(axis)
    return lax.ppermute(value, axis, [(i, (i + step) % size) for i in range(size)])


def on_device(
    tokens,
    key_value_matrix,
    adapter_down_weight,
    adapter_up_weight,
    adapter_store_slot,
    request_adapter,
    prefill_span_pages,
    decode_pool_slot,
):
    pd_count = lax.axis_size("pd")
    st_count = lax.axis_size("st")
    pd_index = lax.axis_index("pd")
    st_index = lax.axis_index("st")
    groups = pd_count * st_count
    me = pd_index * st_count + st_index
    adapter_rank_value = adapter_up_weight.shape[1]
    column_range = adapter_up_weight.shape[2]
    requests = request_adapter.shape[1]
    slot_capacity = requests // groups + 1
    holding_count = adapter_down_weight.shape[0]
    token_rows = tokens.shape[0]
    page_count = token_rows // PAGE_TOKENS

    asked = jnp.concatenate([request_adapter, prefill_span_pages], axis=1)
    asked_by_step = [asked] + [shifted(asked, "pd", step) for step in range(1, pd_count)]
    tokens, asked_by_step = lax.optimization_barrier((tokens, asked_by_step))
    asked_steps = jnp.stack(asked_by_step)
    asked_turns = jnp.stack(
        [asked_steps] + [shifted(asked_steps, "st", turn) for turn in range(1, st_count)], axis=1
    )

    travelled = {(0, 0): tokens}
    for turn in range(1, st_count):
        travelled[0, turn] = shifted(tokens, "st", turn)
    for step in range(1, pd_count):
        travelled[step, 0] = shifted(tokens, "pd", step)

    tokens, asked_turns, near_other = lax.optimization_barrier(
        (tokens, asked_turns, [travelled[0, turn] for turn in range(1, st_count)])
    )
    for turn in range(1, st_count):
        travelled[0, turn] = near_other[turn - 1]
    base_part = jnp.dot(tokens, key_value_matrix, preferred_element_type=jnp.float32)
    base_part, asked_turns = lax.optimization_barrier((base_part.astype(jnp.bfloat16), asked_turns))
    base_sum = lax.psum_scatter(base_part, "tp", scatter_dimension=1, tiled=True)

    by_pd = jnp.take(
        asked_turns, (pd_index - jnp.arange(pd_count)) % pd_count, axis=0, mode="clip"
    )
    asked = jnp.take(
        by_pd, (st_index - jnp.arange(st_count)) % st_count, axis=1, mode="clip"
    ).reshape(groups, 2 * requests)
    store_slot = jnp.take(adapter_store_slot, asked[:, :requests])
    counts = asked[:, requests:]
    ends = jnp.cumsum(counts, axis=1)
    starts = ends - counts
    holder = store_slot // holding_count
    local_index = store_slot % holding_count
    own_slot = jnp.where(holder == me, local_index, -1)

    order_ids = jnp.arange(requests)
    earlier = (holder[:, None, :] == holder[:, :, None]) & (
        order_ids[None, None, :] < order_ids[None, :, None]
    )
    rank_in = jnp.sum(earlier.astype(jnp.int32), axis=2)
    hits = (holder == me)[:, :, None] & (
        rank_in[:, :, None] == jnp.arange(slot_capacity)[None, None, :]
    )
    asked_pages = jnp.sum(jnp.where(hits, local_index[:, :, None], 0), axis=1).reshape(-1)
    up_page_list = jnp.take(adapter_up_weight, asked_pages, axis=0, mode="clip").reshape(
        groups, slot_capacity, adapter_rank_value, column_range
    )
    arrived_up = lax.all_to_all(
        up_page_list, ("pd", "st"), split_axis=0, concat_axis=0, tiled=True
    )
    own_holder = lax.dynamic_index_in_dim(holder, me, 0, keepdims=False)
    own_rank = lax.dynamic_index_in_dim(rank_in, me, 0, keepdims=False)
    own_ends = lax.dynamic_index_in_dim(ends, me, 0, keepdims=False)
    request_of_page = jnp.sum(
        (own_ends[None, :] <= jnp.arange(page_count)[:, None]).astype(jnp.int32), axis=1
    )
    source_of_page = jnp.take(own_holder * slot_capacity + own_rank, request_of_page, mode="clip")
    page_up_weight = jnp.take(
        arrived_up.reshape(groups * slot_capacity, adapter_rank_value, column_range),
        source_of_page,
        axis=0,
        mode="clip",
    )

    def request_tables(step):
        source_group = jnp.stack(
            [
                (pd_index - step) % pd_count * st_count + (st_index - turn) % st_count
                for turn in range(st_count)
            ]
        )
        tables = [
            jnp.take(table, source_group, axis=0, mode="clip")
            for table in (own_slot, starts, counts)
        ]
        return tables

    def summed_products(tables, row_list):
        products = down_products(row_list, *tables, adapter_down_weight)
        chip_sum = products[0]
        for turn in range(1, st_count):
            chip_sum = chip_sum + shifted(products[turn], "st", -turn)
        return chip_sum

    near_rows = [travelled[0, turn] for turn in range(st_count)]
    inner = summed_products(request_tables(0), near_rows).astype(jnp.float32)
    far_tables = [request_tables(step) for step in range(1, pd_count)]
    far_rows = [travelled[step, 0] for step in range(1, pd_count)]
    inner, page_up_weight, base_sum, far_tables, far_rows = lax.optimization_barrier(
        (inner, page_up_weight, base_sum, far_tables, far_rows)
    )
    for step in range(1, pd_count):
        rows = far_rows[step - 1]
        row_list = [rows] + [shifted(rows, "st", turn) for turn in range(1, st_count)]
        returned = shifted(summed_products(far_tables[step - 1], row_list), "pd", -step)
        inner = inner + returned

    tp_count = lax.axis_size("tp")
    half_tensor_parallel = tp_count // 2
    upper = lax.axis_index("tp") >= half_tensor_parallel
    half_rows = token_rows // 2

    def packed(columns):
        return jnp.concatenate([columns[:half_rows], columns[half_rows:]], axis=1)

    first, second = packed(inner[:, :adapter_rank_value]), packed(inner[:, adapter_rank_value:])
    mine = jnp.where(upper, second, first)
    theirs = jnp.where(upper, first, second).astype(jnp.bfloat16)
    mine = mine + shifted(theirs, "tp", half_tensor_parallel)
    distance = half_tensor_parallel // 2
    while distance >= 1:
        pairs = [(i, i ^ distance) for i in range(tp_count)]
        mine = mine + lax.ppermute(mine.astype(jnp.bfloat16), "tp", pairs)
        distance //= 2
    mine = mine.astype(jnp.bfloat16)
    adapter_halfway = jnp.concatenate(
        [mine[:, :adapter_rank_value], mine[:, adapter_rank_value:]], axis=0
    ).reshape(page_count, PAGE_TOKENS, adapter_rank_value)
    update = jnp.einsum(
        "ueo,uox->uex", adapter_halfway, page_up_weight, preferred_element_type=jnp.float32
    )
    completed = base_sum.astype(jnp.float32).reshape(update.shape) + adapter_scale * update
    pages = completed.astype(jnp.bfloat16).reshape(page_count, PAGE_TOKENS * column_range)

    slot_table = decode_pool_slot.reshape(pd_count, st_count, page_count)
    slot_table = lax.dynamic_index_in_dim(slot_table, st_index, 1, keepdims=False)
    own_slots = me * page_count + jnp.arange(page_count)
    decode_pool = None
    for step in range(pd_count):
        arrived = pages if step == 0 else shifted(pages, "pd", step)
        dest = lax.dynamic_index_in_dim(
            slot_table, (pd_index - step) % pd_count, 0, keepdims=False
        )
        selector = (dest[None, :] == own_slots[:, None]).astype(jnp.bfloat16)
        picked = jnp.dot(selector, arrived, preferred_element_type=jnp.float32)
        decode_pool = picked if decode_pool is None else decode_pool + picked
    return decode_pool.astype(jnp.bfloat16).reshape(page_count, PAGE_TOKENS, column_range)


def solution(mesh):
    placed = (
        P(("rep", "pd", "st"), "tp"),
        P("tp", None),
        P(("rep", "pd", "st"), "tp", None),
        P(("rep", "pd", "st"), None, "tp"),
        P("rep"),
        P(("rep", "pd", "st"), None),
        P(("rep", "pd", "st"), None),
        P("rep", None),
    )
    return jax.shard_map(
        on_device,
        mesh=mesh,
        in_specs=placed,
        out_specs=P(("rep", "pd", "st"), None, "tp"),
        check_vma=False,
    )
```

```python
import functools

import jax
import jax.numpy as jnp
from jax import lax
from jax.experimental import pallas as pl
from jax.experimental.pallas import tpu as pltpu
from jax.sharding import PartitionSpec as P

PAGE_TOKENS = 16
CHUNK_PAGES = 8


adapter_scale = 0.5


def down_kernel(sources, requests, slots, starts, counts, down, *refs):
    rows, outs = refs[:sources], refs[sources:]
    page_count = rows[0].shape[0] // PAGE_TOKENS
    chunk_rows = CHUNK_PAGES * PAGE_TOKENS
    for source in range(sources):
        outs[source][...] = jnp.zeros_like(outs[source])

        @pl.loop(0, requests)
        def _(request):
            slot = slots[source, request]
            start = starts[source, request]
            count = counts[source, request]

            @pl.when(slot >= 0)
            def _():
                @pl.loop(0, (count + CHUNK_PAGES - 1) // CHUNK_PAGES)
                def _(chunk):
                    first = jnp.minimum(start + chunk * CHUNK_PAGES, page_count - CHUNK_PAGES)
                    place = pl.ds(pl.multiple_of(first * PAGE_TOKENS, PAGE_TOKENS), chunk_rows)
                    product = jnp.dot(
                        rows[source][place, :], down[slot], preferred_element_type=jnp.float32
                    )
                    row = first * PAGE_TOKENS + lax.broadcasted_iota(jnp.int32, product.shape, 0)
                    inside = (row >= start * PAGE_TOKENS) & (row < (start + count) * PAGE_TOKENS)
                    held = outs[source][place, :].astype(jnp.float32)
                    outs[source][place, :] = jnp.where(inside, product, held).astype(jnp.bfloat16)


def down_products(row_list, slots, starts, counts, down):
    sources, requests = slots.shape
    token_rows, width = row_list[0].shape
    rank = down.shape[2]
    in_vmem = pl.BlockSpec(memory_space=pltpu.VMEM)
    in_smem = pl.BlockSpec(memory_space=pltpu.SMEM)
    return pl.pallas_call(
        functools.partial(down_kernel, sources, requests),
        out_shape=[jax.ShapeDtypeStruct((token_rows, rank), jnp.bfloat16)] * sources,
        in_specs=[in_smem] * 3 + [in_vmem] * (1 + sources),
        out_specs=[in_vmem] * sources,
        compiler_params=pltpu.CompilerParams(vmem_limit_bytes=40 * 1024 * 1024),
        cost_estimate=pl.CostEstimate(
            flops=2 * sources * token_rows * width * rank,
            bytes_accessed=2 * (down.size + sources * token_rows * (width + rank)),
            transcendentals=0,
        ),
        name="down_products",
    )(slots, starts, counts, down, *row_list)


def shifted(value, axis, step):
    size = lax.axis_size(axis)
    return lax.ppermute(value, axis, [(i, (i + step) % size) for i in range(size)])


def on_device(
    tokens,
    key_value_matrix,
    adapter_down_weight,
    adapter_up_weight,
    adapter_store_slot,
    request_adapter,
    prefill_span_pages,
    decode_pool_slot,
):
    pd_count = lax.axis_size("pd")
    st_count = lax.axis_size("st")
    pd_index = lax.axis_index("pd")
    st_index = lax.axis_index("st")
    groups = pd_count * st_count
    me = pd_index * st_count + st_index
    adapter_rank_value = adapter_up_weight.shape[1]
    column_range = adapter_up_weight.shape[2]
    requests = request_adapter.shape[1]
    slot_capacity = requests // groups + 1
    holding_count = adapter_down_weight.shape[0]
    token_rows = tokens.shape[0]
    page_count = token_rows // PAGE_TOKENS

    asked = jnp.concatenate([request_adapter, prefill_span_pages], axis=1)
    asked_by_step = [asked] + [shifted(asked, "pd", step) for step in range(1, pd_count)]
    tokens, asked_by_step = lax.optimization_barrier((tokens, asked_by_step))
    asked_steps = jnp.stack(asked_by_step)
    asked_turns = jnp.stack(
        [asked_steps] + [shifted(asked_steps, "st", turn) for turn in range(1, st_count)], axis=1
    )

    half_rows = token_rows // 2
    far_steps = range(1, pd_count)
    first_half = [shifted(tokens[:half_rows], "pd", step) for step in far_steps]
    base_part = jnp.dot(tokens, key_value_matrix, preferred_element_type=jnp.float32)
    base_part = base_part.astype(jnp.bfloat16)
    near_rows = [tokens] + [shifted(tokens, "st", turn) for turn in range(1, st_count)]
    near_rows, first_half, after_base, asked_turns = lax.optimization_barrier(
        (near_rows, first_half, base_part, asked_turns)
    )
    base_sum = lax.psum_scatter(after_base, "tp", scatter_dimension=1, tiled=True)
    second_half = [shifted(near_rows[0][half_rows:], "pd", step) for step in far_steps]
    first_rows = [
        [rows] + [shifted(rows, "st", turn) for turn in range(1, st_count)] for rows in first_half
    ]

    by_pd = jnp.take(
        asked_turns, (pd_index - jnp.arange(pd_count)) % pd_count, axis=0, mode="clip"
    )
    asked = jnp.take(
        by_pd, (st_index - jnp.arange(st_count)) % st_count, axis=1, mode="clip"
    ).reshape(groups, 2 * requests)
    store_slot = jnp.take(adapter_store_slot, asked[:, :requests])
    counts = asked[:, requests:]
    ends = jnp.cumsum(counts, axis=1)
    starts = ends - counts
    holder = store_slot // holding_count
    local_index = store_slot % holding_count
    own_slot = jnp.where(holder == me, local_index, -1)

    order_ids = jnp.arange(requests)
    earlier = (holder[:, None, :] == holder[:, :, None]) & (
        order_ids[None, None, :] < order_ids[None, :, None]
    )
    rank_in = jnp.sum(earlier.astype(jnp.int32), axis=2)
    hits = (holder == me)[:, :, None] & (
        rank_in[:, :, None] == jnp.arange(slot_capacity)[None, None, :]
    )
    asked_pages = jnp.sum(jnp.where(hits, local_index[:, :, None], 0), axis=1).reshape(-1)
    up_page_list = jnp.take(adapter_up_weight, asked_pages, axis=0, mode="clip").reshape(
        groups, slot_capacity, adapter_rank_value, column_range
    )
    own_holder = lax.dynamic_index_in_dim(holder, me, 0, keepdims=False)
    own_rank = lax.dynamic_index_in_dim(rank_in, me, 0, keepdims=False)
    own_ends = lax.dynamic_index_in_dim(ends, me, 0, keepdims=False)
    request_of_page = jnp.sum(
        (own_ends[None, :] <= jnp.arange(page_count)[:, None]).astype(jnp.int32), axis=1
    )
    source_of_page = jnp.take(own_holder * slot_capacity + own_rank, request_of_page, mode="clip")
    def request_tables(step):
        source_group = jnp.stack(
            [
                (pd_index - step) % pd_count * st_count + (st_index - turn) % st_count
                for turn in range(st_count)
            ]
        )
        tables = [
            jnp.take(table, source_group, axis=0, mode="clip")
            for table in (own_slot, starts, counts)
        ]
        return tables

    def summed_products(tables, row_list, bounds):
        slots, firsts, lengths = tables
        pieces = len(bounds) - 1
        held_first, held_length = [], []
        for low, high in zip(bounds[:-1], bounds[1:]):
            first = jnp.clip(firsts, low, high)
            held_first.append(first - low)
            held_length.append(jnp.clip(firsts + lengths, low, high) - first)
        products = down_products(
            [piece for rows in row_list for piece in rows],
            jnp.repeat(slots, pieces, axis=0),
            jnp.stack(held_first, axis=1).reshape(-1, requests),
            jnp.stack(held_length, axis=1).reshape(-1, requests),
            adapter_down_weight,
        )
        by_turn = [
            jnp.concatenate(products[turn * pieces : (turn + 1) * pieces], axis=0)
            for turn in range(st_count)
        ]
        chip_sum = by_turn[0]
        for turn in range(1, st_count):
            chip_sum = chip_sum + shifted(by_turn[turn], "st", -turn)
        return chip_sum

    whole = token_rows // PAGE_TOKENS
    inner = summed_products(request_tables(0), [[rows] for rows in near_rows], [0, whole])
    inner = inner.astype(jnp.float32)
    far_tables = [request_tables(step) for step in far_steps]
    inner, up_page_list, base_sum, far_tables, first_rows, second_half = lax.optimization_barrier(
        (inner, up_page_list, base_sum, far_tables, first_rows, second_half)
    )
    for step in far_steps:
        rows = second_half[step - 1]
        second_rows = [rows] + [shifted(rows, "st", turn) for turn in range(1, st_count)]
        row_list = [list(halves) for halves in zip(first_rows[step - 1], second_rows)]
        far_sum = summed_products(far_tables[step - 1], row_list, [0, whole // 2, whole])
        inner = inner + shifted(far_sum, "pd", -step)
    arrived_up = lax.all_to_all(
        up_page_list, ("pd", "st"), split_axis=0, concat_axis=0, tiled=True
    )
    page_up_weight = jnp.take(
        arrived_up.reshape(groups * slot_capacity, adapter_rank_value, column_range),
        source_of_page,
        axis=0,
        mode="clip",
    )

    tp_count = lax.axis_size("tp")
    half_tensor_parallel = tp_count // 2
    upper = lax.axis_index("tp") >= half_tensor_parallel

    def packed(columns):
        return jnp.concatenate([columns[:half_rows], columns[half_rows:]], axis=1)

    first, second = packed(inner[:, :adapter_rank_value]), packed(inner[:, adapter_rank_value:])
    mine = jnp.where(upper, second, first)
    theirs = jnp.where(upper, first, second).astype(jnp.bfloat16)
    mine = mine + shifted(theirs, "tp", half_tensor_parallel)
    distance = half_tensor_parallel // 2
    while distance >= 1:
        pairs = [(i, i ^ distance) for i in range(tp_count)]
        mine = mine + lax.ppermute(mine.astype(jnp.bfloat16), "tp", pairs)
        distance //= 2
    mine = mine.astype(jnp.bfloat16)
    adapter_halfway = jnp.concatenate(
        [mine[:, :adapter_rank_value], mine[:, adapter_rank_value:]], axis=0
    ).reshape(page_count, PAGE_TOKENS, adapter_rank_value)
    update = jnp.einsum(
        "ueo,uox->uex", adapter_halfway, page_up_weight, preferred_element_type=jnp.float32
    )
    completed = base_sum.astype(jnp.float32).reshape(update.shape) + adapter_scale * update
    pages = completed.astype(jnp.bfloat16).reshape(page_count, PAGE_TOKENS * column_range)

    slot_table = decode_pool_slot.reshape(pd_count, st_count, page_count)
    slot_table = lax.dynamic_index_in_dim(slot_table, st_index, 1, keepdims=False)
    own_slots = me * page_count + jnp.arange(page_count)
    decode_pool = None
    for step in range(pd_count):
        arrived = pages if step == 0 else shifted(pages, "pd", step)
        dest = lax.dynamic_index_in_dim(
            slot_table, (pd_index - step) % pd_count, 0, keepdims=False
        )
        selector = (dest[None, :] == own_slots[:, None]).astype(jnp.bfloat16)
        picked = jnp.dot(selector, arrived, preferred_element_type=jnp.float32)
        decode_pool = picked if decode_pool is None else decode_pool + picked
    return decode_pool.astype(jnp.bfloat16).reshape(page_count, PAGE_TOKENS, column_range)


def solution(mesh):
    placed = (
        P(("rep", "pd", "st"), "tp"),
        P("tp", None),
        P(("rep", "pd", "st"), "tp", None),
        P(("rep", "pd", "st"), None, "tp"),
        P("rep"),
        P(("rep", "pd", "st"), None),
        P(("rep", "pd", "st"), None),
        P("rep", None),
    )
    return jax.shard_map(
        on_device,
        mesh=mesh,
        in_specs=placed,
        out_specs=P(("rep", "pd", "st"), None, "tp"),
        check_vma=False,
    )
```

```python
import functools

import jax
import jax.numpy as jnp
from jax import lax
from jax.experimental import pallas as pl
from jax.experimental.pallas import tpu as pltpu
from jax.sharding import PartitionSpec as P

PAGE_TOKENS = 16
CHUNK_PAGES = 8


adapter_scale = 0.5


def down_kernel(sources, requests, slots, starts, counts, down, *refs):
    rows, outs = refs[:sources], refs[sources:]
    assert min(piece.shape[0] for piece in rows) >= CHUNK_PAGES * PAGE_TOKENS
    chunk_rows = CHUNK_PAGES * PAGE_TOKENS
    for source in range(sources):
        page_count = rows[source].shape[0] // PAGE_TOKENS
        outs[source][...] = jnp.zeros_like(outs[source])

        @pl.loop(0, requests)
        def _(request):
            slot = slots[source, request]
            start = starts[source, request]
            count = counts[source, request]

            @pl.when(slot >= 0)
            def _():
                @pl.loop(0, (count + CHUNK_PAGES - 1) // CHUNK_PAGES)
                def _(chunk):
                    first = jnp.minimum(start + chunk * CHUNK_PAGES, page_count - CHUNK_PAGES)
                    place = pl.ds(pl.multiple_of(first * PAGE_TOKENS, PAGE_TOKENS), chunk_rows)
                    product = jnp.dot(
                        rows[source][place, :], down[slot], preferred_element_type=jnp.float32
                    )
                    row = first * PAGE_TOKENS + lax.broadcasted_iota(jnp.int32, product.shape, 0)
                    inside = (row >= start * PAGE_TOKENS) & (row < (start + count) * PAGE_TOKENS)
                    held = outs[source][place, :].astype(jnp.float32)
                    outs[source][place, :] = jnp.where(inside, product, held).astype(jnp.bfloat16)


def down_products(row_list, slots, starts, counts, down):
    sources, requests = slots.shape
    total_rows = sum(rows.shape[0] for rows in row_list)
    width, rank = down.shape[1:]
    in_vmem = pl.BlockSpec(memory_space=pltpu.VMEM)
    in_smem = pl.BlockSpec(memory_space=pltpu.SMEM)
    return pl.pallas_call(
        functools.partial(down_kernel, sources, requests),
        out_shape=[
            jax.ShapeDtypeStruct((rows.shape[0], rank), jnp.bfloat16) for rows in row_list
        ],
        in_specs=[in_smem] * 3 + [in_vmem] * (1 + sources),
        out_specs=[in_vmem] * sources,
        compiler_params=pltpu.CompilerParams(vmem_limit_bytes=40 * 1024 * 1024),
        cost_estimate=pl.CostEstimate(
            flops=2 * total_rows * width * rank,
            bytes_accessed=2 * (down.size + total_rows * (width + rank)),
            transcendentals=0,
        ),
        name="down_products",
    )(slots, starts, counts, down, *row_list)


def shifted(value, axis, step):
    size = lax.axis_size(axis)
    return lax.ppermute(value, axis, [(i, (i + step) % size) for i in range(size)])


def on_device(
    tokens,
    key_value_matrix,
    adapter_down_weight,
    adapter_up_weight,
    adapter_store_slot,
    request_adapter,
    prefill_span_pages,
    decode_pool_slot,
):
    pd_count = lax.axis_size("pd")
    st_count = lax.axis_size("st")
    pd_index = lax.axis_index("pd")
    st_index = lax.axis_index("st")
    groups = pd_count * st_count
    me = pd_index * st_count + st_index
    adapter_rank_value = adapter_up_weight.shape[1]
    column_range = adapter_up_weight.shape[2]
    requests = request_adapter.shape[1]
    slot_capacity = requests // groups + 1
    holding_count = adapter_down_weight.shape[0]
    token_rows = tokens.shape[0]
    page_count = token_rows // PAGE_TOKENS

    asked = jnp.concatenate([request_adapter, prefill_span_pages], axis=1)
    asked_by_step = [asked] + [shifted(asked, "pd", step) for step in range(1, pd_count)]
    tokens, asked_by_step = lax.optimization_barrier((tokens, asked_by_step))
    asked_steps = jnp.stack(asked_by_step)
    asked_turns = jnp.stack(
        [asked_steps] + [shifted(asked_steps, "st", turn) for turn in range(1, st_count)], axis=1
    )

    half_rows = token_rows // 2
    first_count = token_rows // 4
    far_steps = range(1, pd_count)
    first_piece = [shifted(tokens[:first_count], "pd", step) for step in far_steps]
    base_part = jnp.dot(tokens, key_value_matrix, preferred_element_type=jnp.float32)
    base_part = base_part.astype(jnp.bfloat16)
    near_rows = [tokens] + [shifted(tokens, "st", turn) for turn in range(1, st_count)]
    near_rows, first_piece, after_base, asked_turns, rest = lax.optimization_barrier(
        (near_rows, first_piece, base_part, asked_turns, tokens[first_count:])
    )
    base_sum = lax.psum_scatter(after_base, "tp", scatter_dimension=1, tiled=True)
    second_piece = [shifted(rest, "pd", step) for step in far_steps]
    first_rows = [
        [rows] + [shifted(rows, "st", turn) for turn in range(1, st_count)] for rows in first_piece
    ]

    by_pd = jnp.take(
        asked_turns, (pd_index - jnp.arange(pd_count)) % pd_count, axis=0, mode="clip"
    )
    asked = jnp.take(
        by_pd, (st_index - jnp.arange(st_count)) % st_count, axis=1, mode="clip"
    ).reshape(groups, 2 * requests)
    store_slot = jnp.take(adapter_store_slot, asked[:, :requests])
    counts = asked[:, requests:]
    ends = jnp.cumsum(counts, axis=1)
    starts = ends - counts
    holder = store_slot // holding_count
    local_index = store_slot % holding_count
    own_slot = jnp.where(holder == me, local_index, -1)

    order_ids = jnp.arange(requests)
    earlier = (holder[:, None, :] == holder[:, :, None]) & (
        order_ids[None, None, :] < order_ids[None, :, None]
    )
    rank_in = jnp.sum(earlier.astype(jnp.int32), axis=2)
    hits = (holder == me)[:, :, None] & (
        rank_in[:, :, None] == jnp.arange(slot_capacity)[None, None, :]
    )
    asked_pages = jnp.sum(jnp.where(hits, local_index[:, :, None], 0), axis=1).reshape(-1)
    up_page_list = jnp.take(adapter_up_weight, asked_pages, axis=0, mode="clip").reshape(
        groups, slot_capacity, adapter_rank_value, column_range
    )
    own_holder = lax.dynamic_index_in_dim(holder, me, 0, keepdims=False)
    own_rank = lax.dynamic_index_in_dim(rank_in, me, 0, keepdims=False)
    own_ends = lax.dynamic_index_in_dim(ends, me, 0, keepdims=False)
    request_of_page = jnp.sum(
        (own_ends[None, :] <= jnp.arange(page_count)[:, None]).astype(jnp.int32), axis=1
    )
    source_of_page = jnp.take(own_holder * slot_capacity + own_rank, request_of_page, mode="clip")
    def request_tables(step):
        source_group = jnp.stack(
            [
                (pd_index - step) % pd_count * st_count + (st_index - turn) % st_count
                for turn in range(st_count)
            ]
        )
        tables = [
            jnp.take(table, source_group, axis=0, mode="clip")
            for table in (own_slot, starts, counts)
        ]
        return tables

    def summed_products(tables, row_list, bounds):
        slots, firsts, lengths = tables
        pieces = len(bounds) - 1
        held_first, held_length = [], []
        for low, high in zip(bounds[:-1], bounds[1:]):
            first = jnp.clip(firsts, low, high)
            held_first.append(first - low)
            held_length.append(jnp.clip(firsts + lengths, low, high) - first)
        products = down_products(
            [piece for rows in row_list for piece in rows],
            jnp.repeat(slots, pieces, axis=0),
            jnp.stack(held_first, axis=1).reshape(-1, requests),
            jnp.stack(held_length, axis=1).reshape(-1, requests),
            adapter_down_weight,
        )
        by_turn = [
            jnp.concatenate(products[turn * pieces : (turn + 1) * pieces], axis=0)
            for turn in range(st_count)
        ]
        chip_sum = by_turn[0]
        for turn in range(1, st_count):
            chip_sum = chip_sum + shifted(by_turn[turn], "st", -turn)
        return chip_sum

    whole = token_rows // PAGE_TOKENS
    inner = summed_products(request_tables(0), [[rows] for rows in near_rows], [0, whole])
    inner = inner.astype(jnp.float32)
    far_tables = [request_tables(step) for step in far_steps]
    inner, up_page_list, base_sum, far_tables, first_rows, second_piece = lax.optimization_barrier(
        (inner, up_page_list, base_sum, far_tables, first_rows, second_piece)
    )
    far_sums = []
    for step in far_steps:
        rows = second_piece[step - 1]
        second_rows = [rows] + [shifted(rows, "st", turn) for turn in range(1, st_count)]
        row_list = [list(pieces) for pieces in zip(first_rows[step - 1], second_rows)]
        far_sums.append(
            summed_products(
                far_tables[step - 1], row_list, [0, first_count // PAGE_TOKENS, whole]
            )
        )
    arrived_up = lax.all_to_all(
        up_page_list, ("pd", "st"), split_axis=0, concat_axis=0, tiled=True
    )
    page_up_weight = jnp.take(
        arrived_up.reshape(groups * slot_capacity, adapter_rank_value, column_range),
        source_of_page,
        axis=0,
        mode="clip",
    )
    far_sums, page_up_weight = lax.optimization_barrier((far_sums, page_up_weight))
    for step in far_steps:
        inner = inner + shifted(far_sums[step - 1], "pd", -step)

    tp_count = lax.axis_size("tp")
    half_tensor_parallel = tp_count // 2
    upper = lax.axis_index("tp") >= half_tensor_parallel

    def packed(columns):
        return jnp.concatenate([columns[:half_rows], columns[half_rows:]], axis=1)

    first, second = packed(inner[:, :adapter_rank_value]), packed(inner[:, adapter_rank_value:])
    mine = jnp.where(upper, second, first)
    theirs = jnp.where(upper, first, second).astype(jnp.bfloat16)
    mine = mine + shifted(theirs, "tp", half_tensor_parallel)
    distance = half_tensor_parallel // 2
    while distance >= 1:
        pairs = [(i, i ^ distance) for i in range(tp_count)]
        mine = mine + lax.ppermute(mine.astype(jnp.bfloat16), "tp", pairs)
        distance //= 2
    mine = mine.astype(jnp.bfloat16)
    adapter_halfway = jnp.concatenate(
        [mine[:, :adapter_rank_value], mine[:, adapter_rank_value:]], axis=0
    ).reshape(page_count, PAGE_TOKENS, adapter_rank_value)
    update = jnp.einsum(
        "ueo,uox->uex", adapter_halfway, page_up_weight, preferred_element_type=jnp.float32
    )
    completed = base_sum.astype(jnp.float32).reshape(update.shape) + adapter_scale * update
    pages = completed.astype(jnp.bfloat16).reshape(page_count, PAGE_TOKENS * column_range)

    slot_table = decode_pool_slot.reshape(pd_count, st_count, page_count)
    slot_table = lax.dynamic_index_in_dim(slot_table, st_index, 1, keepdims=False)
    own_slots = me * page_count + jnp.arange(page_count)
    decode_pool = None
    for step in range(pd_count):
        arrived = pages if step == 0 else shifted(pages, "pd", step)
        dest = lax.dynamic_index_in_dim(
            slot_table, (pd_index - step) % pd_count, 0, keepdims=False
        )
        selector = (dest[None, :] == own_slots[:, None]).astype(jnp.bfloat16)
        picked = jnp.dot(selector, arrived, preferred_element_type=jnp.float32)
        decode_pool = picked if decode_pool is None else decode_pool + picked
    return decode_pool.astype(jnp.bfloat16).reshape(page_count, PAGE_TOKENS, column_range)


def solution(mesh):
    placed = (
        P(("rep", "pd", "st"), "tp"),
        P("tp", None),
        P(("rep", "pd", "st"), "tp", None),
        P(("rep", "pd", "st"), None, "tp"),
        P("rep"),
        P(("rep", "pd", "st"), None),
        P(("rep", "pd", "st"), None),
        P("rep", None),
    )
    return jax.shard_map(
        on_device,
        mesh=mesh,
        in_specs=placed,
        out_specs=P(("rep", "pd", "st"), None, "tp"),
        check_vma=False,
    )
```

```python
import functools

import jax
import jax.numpy as jnp
from jax import lax
from jax.experimental import pallas as pl
from jax.experimental.pallas import tpu as pltpu
from jax.sharding import PartitionSpec as P

PAGE_TOKENS = 16
CHUNK_PAGES = 8


adapter_scale = 0.5


def down_kernel(sources, requests, slots, starts, counts, down, *refs):
    rows, outs = refs[:sources], refs[sources:]
    assert min(piece.shape[0] for piece in rows) >= CHUNK_PAGES * PAGE_TOKENS
    chunk_rows = CHUNK_PAGES * PAGE_TOKENS
    for source in range(sources):
        page_count = rows[source].shape[0] // PAGE_TOKENS
        outs[source][...] = jnp.zeros_like(outs[source])

        @pl.loop(0, requests)
        def _(request):
            slot = slots[source, request]
            start = starts[source, request]
            count = counts[source, request]

            @pl.when(slot >= 0)
            def _():
                @pl.loop(0, (count + CHUNK_PAGES - 1) // CHUNK_PAGES)
                def _(chunk):
                    first = jnp.minimum(start + chunk * CHUNK_PAGES, page_count - CHUNK_PAGES)
                    place = pl.ds(pl.multiple_of(first * PAGE_TOKENS, PAGE_TOKENS), chunk_rows)
                    product = jnp.dot(
                        rows[source][place, :], down[slot], preferred_element_type=jnp.float32
                    )
                    row = first * PAGE_TOKENS + lax.broadcasted_iota(jnp.int32, product.shape, 0)
                    inside = (row >= start * PAGE_TOKENS) & (row < (start + count) * PAGE_TOKENS)
                    held = outs[source][place, :].astype(jnp.float32)
                    outs[source][place, :] = jnp.where(inside, product, held).astype(jnp.bfloat16)


def down_products(row_list, slots, starts, counts, down):
    sources, requests = slots.shape
    total_rows = sum(rows.shape[0] for rows in row_list)
    width, rank = down.shape[1:]
    in_vmem = pl.BlockSpec(memory_space=pltpu.VMEM)
    in_smem = pl.BlockSpec(memory_space=pltpu.SMEM)
    return pl.pallas_call(
        functools.partial(down_kernel, sources, requests),
        out_shape=[
            jax.ShapeDtypeStruct((rows.shape[0], rank), jnp.bfloat16) for rows in row_list
        ],
        in_specs=[in_smem] * 3 + [in_vmem] * (1 + sources),
        out_specs=[in_vmem] * sources,
        compiler_params=pltpu.CompilerParams(vmem_limit_bytes=40 * 1024 * 1024),
        cost_estimate=pl.CostEstimate(
            flops=2 * total_rows * width * rank,
            bytes_accessed=2 * (down.size + total_rows * (width + rank)),
            transcendentals=0,
        ),
        name="down_products",
    )(slots, starts, counts, down, *row_list)


def shifted(value, axis, step):
    size = lax.axis_size(axis)
    return lax.ppermute(value, axis, [(i, (i + step) % size) for i in range(size)])


def on_device(
    tokens,
    key_value_matrix,
    adapter_down_weight,
    adapter_up_weight,
    adapter_store_slot,
    request_adapter,
    prefill_span_pages,
    decode_pool_slot,
):
    pd_count = lax.axis_size("pd")
    st_count = lax.axis_size("st")
    pd_index = lax.axis_index("pd")
    st_index = lax.axis_index("st")
    groups = pd_count * st_count
    me = pd_index * st_count + st_index
    adapter_rank_value = adapter_up_weight.shape[1]
    column_range = adapter_up_weight.shape[2]
    requests = request_adapter.shape[1]
    slot_capacity = requests // groups + 1
    holding_count = adapter_down_weight.shape[0]
    token_rows = tokens.shape[0]
    page_count = token_rows // PAGE_TOKENS

    asked = jnp.concatenate([request_adapter, prefill_span_pages], axis=1)
    asked_by_step = [asked] + [shifted(asked, "pd", step) for step in range(1, pd_count)]
    tokens, asked_by_step = lax.optimization_barrier((tokens, asked_by_step))
    asked_steps = jnp.stack(asked_by_step)
    asked_turns = jnp.stack(
        [asked_steps] + [shifted(asked_steps, "st", turn) for turn in range(1, st_count)], axis=1
    )

    half_rows = token_rows // 2
    first_count = token_rows // 4
    far_steps = range(1, pd_count)
    first_piece = [shifted(tokens[:first_count], "pd", step) for step in far_steps]
    base_part = jnp.dot(tokens, key_value_matrix, preferred_element_type=jnp.float32)
    base_part = base_part.astype(jnp.bfloat16)
    near_rows = [tokens] + [shifted(tokens, "st", turn) for turn in range(1, st_count)]
    near_rows, first_piece, after_base, asked_turns, rest = lax.optimization_barrier(
        (near_rows, first_piece, base_part, asked_turns, tokens[first_count:])
    )
    early_count = token_rows - first_count
    base_sum = lax.psum_scatter(
        after_base[:early_count], "tp", scatter_dimension=1, tiled=True
    )
    late_sum = lax.psum_scatter(
        after_base[early_count:], "tp", scatter_dimension=1, tiled=True
    )
    second_piece = [shifted(rest, "pd", step) for step in far_steps]
    first_rows = [
        [rows] + [shifted(rows, "st", turn) for turn in range(1, st_count)] for rows in first_piece
    ]

    by_pd = jnp.take(
        asked_turns, (pd_index - jnp.arange(pd_count)) % pd_count, axis=0, mode="clip"
    )
    asked = jnp.take(
        by_pd, (st_index - jnp.arange(st_count)) % st_count, axis=1, mode="clip"
    ).reshape(groups, 2 * requests)
    store_slot = jnp.take(adapter_store_slot, asked[:, :requests])
    counts = asked[:, requests:]
    ends = jnp.cumsum(counts, axis=1)
    starts = ends - counts
    holder = store_slot // holding_count
    local_index = store_slot % holding_count
    own_slot = jnp.where(holder == me, local_index, -1)

    order_ids = jnp.arange(requests)
    earlier = (holder[:, None, :] == holder[:, :, None]) & (
        order_ids[None, None, :] < order_ids[None, :, None]
    )
    rank_in = jnp.sum(earlier.astype(jnp.int32), axis=2)
    hits = (holder == me)[:, :, None] & (
        rank_in[:, :, None] == jnp.arange(slot_capacity)[None, None, :]
    )
    asked_pages = jnp.sum(jnp.where(hits, local_index[:, :, None], 0), axis=1).reshape(-1)
    up_page_list = jnp.take(adapter_up_weight, asked_pages, axis=0, mode="clip").reshape(
        groups, slot_capacity, adapter_rank_value, column_range
    )
    own_holder = lax.dynamic_index_in_dim(holder, me, 0, keepdims=False)
    own_rank = lax.dynamic_index_in_dim(rank_in, me, 0, keepdims=False)
    own_ends = lax.dynamic_index_in_dim(ends, me, 0, keepdims=False)
    request_of_page = jnp.sum(
        (own_ends[None, :] <= jnp.arange(page_count)[:, None]).astype(jnp.int32), axis=1
    )
    source_of_page = jnp.take(own_holder * slot_capacity + own_rank, request_of_page, mode="clip")
    def request_tables(step):
        source_group = jnp.stack(
            [
                (pd_index - step) % pd_count * st_count + (st_index - turn) % st_count
                for turn in range(st_count)
            ]
        )
        tables = [
            jnp.take(table, source_group, axis=0, mode="clip")
            for table in (own_slot, starts, counts)
        ]
        return tables

    def summed_products(tables, row_list, bounds):
        slots, firsts, lengths = tables
        pieces = len(bounds) - 1
        held_first, held_length = [], []
        for low, high in zip(bounds[:-1], bounds[1:]):
            first = jnp.clip(firsts, low, high)
            held_first.append(first - low)
            held_length.append(jnp.clip(firsts + lengths, low, high) - first)
        products = down_products(
            [piece for rows in row_list for piece in rows],
            jnp.repeat(slots, pieces, axis=0),
            jnp.stack(held_first, axis=1).reshape(-1, requests),
            jnp.stack(held_length, axis=1).reshape(-1, requests),
            adapter_down_weight,
        )
        by_turn = [
            jnp.concatenate(products[turn * pieces : (turn + 1) * pieces], axis=0)
            for turn in range(st_count)
        ]
        chip_sum = by_turn[0]
        for turn in range(1, st_count):
            chip_sum = chip_sum + shifted(by_turn[turn], "st", -turn)
        return chip_sum

    whole = token_rows // PAGE_TOKENS
    inner = summed_products(request_tables(0), [[rows] for rows in near_rows], [0, whole])
    inner = inner.astype(jnp.float32)
    far_tables = [request_tables(step) for step in far_steps]
    inner, up_page_list, base_sum, far_tables, first_rows, second_piece = lax.optimization_barrier(
        (inner, up_page_list, base_sum, far_tables, first_rows, second_piece)
    )
    far_sums = []
    for step in far_steps:
        rows = second_piece[step - 1]
        second_rows = [rows] + [shifted(rows, "st", turn) for turn in range(1, st_count)]
        row_list = [list(pieces) for pieces in zip(first_rows[step - 1], second_rows)]
        far_sums.append(
            summed_products(
                far_tables[step - 1], row_list, [0, first_count // PAGE_TOKENS, whole]
            )
        )
    arrived_up = lax.all_to_all(
        up_page_list, ("pd", "st"), split_axis=0, concat_axis=0, tiled=True
    )
    page_up_weight = jnp.take(
        arrived_up.reshape(groups * slot_capacity, adapter_rank_value, column_range),
        source_of_page,
        axis=0,
        mode="clip",
    )
    far_sums, page_up_weight, late_sum = lax.optimization_barrier(
        (far_sums, page_up_weight, late_sum)
    )
    base_sum = jnp.concatenate([base_sum, late_sum], axis=0)
    for step in far_steps:
        inner = inner + shifted(far_sums[step - 1], "pd", -step)

    tp_count = lax.axis_size("tp")
    half_tensor_parallel = tp_count // 2
    upper = lax.axis_index("tp") >= half_tensor_parallel

    def packed(columns):
        return jnp.concatenate([columns[:half_rows], columns[half_rows:]], axis=1)

    first, second = packed(inner[:, :adapter_rank_value]), packed(inner[:, adapter_rank_value:])
    mine = jnp.where(upper, second, first)
    theirs = jnp.where(upper, first, second).astype(jnp.bfloat16)
    mine = mine + shifted(theirs, "tp", half_tensor_parallel)
    distance = half_tensor_parallel // 2
    while distance >= 1:
        pairs = [(i, i ^ distance) for i in range(tp_count)]
        mine = mine + lax.ppermute(mine.astype(jnp.bfloat16), "tp", pairs)
        distance //= 2
    mine = mine.astype(jnp.bfloat16)
    adapter_halfway = jnp.concatenate(
        [mine[:, :adapter_rank_value], mine[:, adapter_rank_value:]], axis=0
    ).reshape(page_count, PAGE_TOKENS, adapter_rank_value)
    update = jnp.einsum(
        "ueo,uox->uex", adapter_halfway, page_up_weight, preferred_element_type=jnp.float32
    )
    completed = base_sum.astype(jnp.float32).reshape(update.shape) + adapter_scale * update
    pages = completed.astype(jnp.bfloat16).reshape(page_count, PAGE_TOKENS * column_range)

    slot_table = decode_pool_slot.reshape(pd_count, st_count, page_count)
    slot_table = lax.dynamic_index_in_dim(slot_table, st_index, 1, keepdims=False)
    own_slots = me * page_count + jnp.arange(page_count)
    decode_pool = None
    for step in range(pd_count):
        arrived = pages if step == 0 else shifted(pages, "pd", step)
        dest = lax.dynamic_index_in_dim(
            slot_table, (pd_index - step) % pd_count, 0, keepdims=False
        )
        selector = (dest[None, :] == own_slots[:, None]).astype(jnp.bfloat16)
        picked = jnp.dot(selector, arrived, preferred_element_type=jnp.float32)
        decode_pool = picked if decode_pool is None else decode_pool + picked
    return decode_pool.astype(jnp.bfloat16).reshape(page_count, PAGE_TOKENS, column_range)


def solution(mesh):
    placed = (
        P(("rep", "pd", "st"), "tp"),
        P("tp", None),
        P(("rep", "pd", "st"), "tp", None),
        P(("rep", "pd", "st"), None, "tp"),
        P("rep"),
        P(("rep", "pd", "st"), None),
        P(("rep", "pd", "st"), None),
        P("rep", None),
    )
    return jax.shard_map(
        on_device,
        mesh=mesh,
        in_specs=placed,
        out_specs=P(("rep", "pd", "st"), None, "tp"),
        check_vma=False,
    )
```
